32 devices in a mesh: row: 4 (over z), col: 8 (over y, x, core).
Axes of the slice: x: 2, y: 2, z: 4, core: 2. Of those that a mesh axis runs over, the one named last changes fastest.
Arguments:
- factor_strip: float32 [4, 3, 512, 2048], P(None, None, 'col', 'row'), may hold values from -0.4375 to 0.4375
- pivots: float32 [3, 512], replicated, may hold values from 1 to 4
- right_side: float32 [4, 2048, 8192], P(None, 'row', 'col'), may hold values from -6 to 6
Outputs:
- solved: float32 [3, 512, 8192], P(None, None, 'col')
- trailing: float32 [4, 2048, 8192], P(None, 'row', 'col')
The draws below stay inside these ranges and needn't reach their ends.
All inputs are finite; a program needn't handle non-finite values.
Results may differ from the reference program's by a relative error of at most 0.0001.
Values sent between devices are 32-bit elements; how exact they have to be, the bound alone decides.
A program may use at most 128 MiB of HBM per device.

```python
import math
import jax
import jax.numpy as jnp
from jax import lax

PANEL = 512
PANELS = 3
RB_DEV = 4
M_ROW = 2048
NC = 8192
N_ROW = 4


def steps_of(stream_key, extent, shards, smallest, top_value):
    gain = 1.0
    for position, blocks in shards:
        heights = jax.random.uniform(jax.random.fold_in(jax.random.fold_in(stream_key, 6), position), (blocks,), jnp.float32, smallest / len(shards), top_value / len(shards))
        gain = gain * jnp.repeat(jnp.exp(heights), extent[position] // blocks).reshape((-1,) + (1,) * (len(extent) - 1 - position))
    return gain


def centred(own_key, shape, width, limit, split=(), kind=jnp.bfloat16):
    gain = steps_of(own_key, shape, split, -0.22, 0.18) if split else 1.0
    array = jax.random.normal(own_key, shape, jnp.float32) * width * gain
    return jnp.minimum(jnp.maximum(array, -limit), limit).astype(kind)


def setup_inputs(seed: int = 0) -> dict:
    key_of = jax.random.split(jax.random.key(seed), 4)
    return {
        "factor_strip": centred(key_of[0], (RB_DEV, PANELS, PANEL, M_ROW), 0.03, 0.4375, ((2, 8), (3, 4)), jnp.float32),
        "pivots": jnp.clip(jnp.exp(jax.random.uniform(key_of[1], (PANELS, PANEL), jnp.float32, math.log(1.0), math.log(4.0))), 1.0, 4.0),
        "right_side": centred(key_of[2], (RB_DEV, M_ROW, NC), 1.0, 6.0, ((1, 4), (2, 8)), jnp.float32),
    }


def reference(factor_strip, pivots, right_side):
    blocks = jnp.arange(RB_DEV, dtype=jnp.int32)[:, None] * N_ROW + (jnp.arange(M_ROW, dtype=jnp.int32) // PANEL)[None, :]
    work = right_side
    outputs = []
    for panel_index in range(PANELS):
        panel = factor_strip[:, panel_index]
        square = panel[0, :, panel_index * PANEL:(panel_index + 1) * PANEL].T
        lower = jnp.tril(square, -1) + jnp.diag(pivots[panel_index])
        target = work[0, panel_index * PANEL:(panel_index + 1) * PANEL]
        result = jax.scipy.linalg.solve_triangular(lower, target, lower=True)
        outputs.append(result)
        update = jnp.einsum('bcr,cn->brn', panel, result, precision=lax.Precision.HIGHEST)
        keep = (blocks > panel_index)[:, :, None]
        work = jnp.where(keep, work - update, work)
    return (jnp.stack(outputs), work)
```

```python
import functools

import jax
import jax.numpy as jnp
from jax import lax
from jax.experimental import pallas as pl
from jax.experimental.pallas import tpu as pltpu
from jax.sharding import PartitionSpec as P

BLOCK = 128
BASE = 16
CHUNKS = 2
HIGHEST = lax.Precision.HIGHEST


def split(value):
    high = value.astype(jnp.bfloat16)
    low = (value - high.astype(jnp.float32)).astype(jnp.bfloat16)
    return high, low


def split_words(value):
    high = lax.reduce_precision(value, 8, 7)
    return high.astype(jnp.bfloat16), (value - high).astype(jnp.bfloat16)


def product(a_high, a_low, b_high, b_low):
    dot = functools.partial(jnp.dot, preferred_element_type=jnp.float32)
    return dot(a_high, b_high) + (dot(a_high, b_low) + dot(a_low, b_high))


def block_inverses(lower, diagonal):
    size = lower.shape[-1]
    mul = functools.partial(jnp.matmul, precision=HIGHEST)
    scaled = lower / diagonal[:, :, None]
    index = jnp.arange(size)
    eye = jnp.eye(size, dtype=jnp.float32)

    def same(width):
        return (index[:, None] // width) == (index[None, :] // width)

    power = jnp.where(same(BASE), -scaled, 0.0)
    inverse = eye + power
    width = 2
    while width < BASE:
        power = mul(power, power)
        inverse = inverse + mul(inverse, power)
        width *= 2
    width = BASE
    while width < size:
        off = jnp.where(same(2 * width) & ~same(width), scaled, 0.0)
        inverse = inverse - mul(mul(inverse, off), inverse)
        width *= 2
    return inverse / diagonal[:, None, :]


def chunk_kernel(panels, panel, row_count, tri_h, tri_l, inv_h, inv_l, rhs0, fac_h, fac_l, rhs, *rest):
    solved, trailing, x_high, x_low = rest[-4:]
    step = pl.program_id(0)
    total = panels * panel

    @pl.when(step == 0)
    def _():
        for i in range(total // BLOCK):
            lo, hi = i * BLOCK, (i + 1) * BLOCK
            p, at = lo // panel, lo % panel
            acc = rhs0[p, at:at + BLOCK, :]
            if i:
                acc = acc - product(tri_h[lo:hi, :lo], tri_l[lo:hi, :lo], x_high[:lo, :], x_low[:lo, :])
            a_high, a_low = split(acc)
            x = product(inv_h[i], inv_l[i], a_high, a_low)
            solved[p, at:at + BLOCK, :] = x
            b_high, b_low = split(x)
            x_high[lo:hi, :] = b_high
            x_low[lo:hi, :] = b_low

    @pl.when(step > 0)
    def _():
        trailing[0] = rhs[0] - product(fac_h[0], fac_l[0], x_high[...], x_low[...])


def chunk_call(index, chunks, tri, inv, rhs0, fac, right_side, row_count, previous):
    panels, panel = rhs0.shape[0], rhs0.shape[1]
    sweeps, rows, columns = right_side.shape
    width = columns // chunks
    total = panels * panel
    whole = lambda shape: pl.BlockSpec(shape, lambda s: (0,) * len(shape))
    sweep = lambda s: jnp.maximum(s - 1, 0)
    in_specs = [
        whole((total, total)), whole((total, total)),
        whole(inv[0].shape), whole(inv[1].shape),
        whole(rhs0.shape),
        pl.BlockSpec((1, rows, total), lambda s: (sweep(s), 0, 0)),
        pl.BlockSpec((1, rows, total), lambda s: (sweep(s), 0, 0)),
        pl.BlockSpec((1, rows, width), lambda s: (sweep(s), 0, index)),
    ]
    args = [*tri, *inv, rhs0, *fac, right_side]
    aliases = {}
    if previous is not None:
        in_specs += [pl.BlockSpec(memory_space=pl.ANY)] * 2
        aliases = {len(args): 0, len(args) + 1: 1}
        args += list(previous)
    return pl.pallas_call(
        functools.partial(chunk_kernel, panels, panel, row_count),
        grid=(sweeps + 1,),
        in_specs=in_specs,
        out_specs=[
            pl.BlockSpec((panels, panel, width), lambda s: (0, 0, index)),
            pl.BlockSpec((1, rows, width), lambda s: (sweep(s), 0, index)),
        ],
        out_shape=[
            jax.ShapeDtypeStruct((panels, panel, columns), jnp.float32),
            jax.ShapeDtypeStruct((sweeps, rows, columns), jnp.float32),
        ],
        scratch_shapes=[pltpu.VMEM((total, width), jnp.bfloat16)] * 2,
        input_output_aliases=aliases,
        compiler_params=pltpu.CompilerParams(vmem_limit_bytes=56 * 1024 * 1024),
        cost_estimate=pl.CostEstimate(
            flops=6 * (total * total // 2 + sweeps * rows * total) * width,
            bytes_accessed=4 * (total * total + sweeps * rows * total + 2 * sweeps * rows * width),
            transcendentals=0),
    )(*args)


def per_device(factor_strip, pivots, right_side):
    row_index = lax.axis_index("row")
    row_count = lax.axis_size("row")
    sweeps, rows, columns = right_side.shape
    panels, panel = pivots.shape
    total = panels * panel

    local = lax.all_gather(factor_strip[0], "row", axis=2, tiled=True)
    local = jnp.concatenate([local[p, :, p * panel:total] for p in range(panels)], axis=1)
    shared = lax.all_gather(local, "col", axis=0, tiled=True)
    gathered = lax.all_gather(factor_strip, "col", axis=2, tiled=True)
    width = columns // CHUNKS
    heads = [
        lax.all_gather(right_side[0, :, k * width:(k + 1) * width], "row", axis=0)[:panels]
        for k in range(CHUNKS)
    ]

    parts, at = [], 0
    for p in range(panels):
        tall = total - p * panel
        parts.append(jnp.pad(shared[:, at:at + tall].T, ((p * panel, 0), (0, 0))))
        at += tall
    full = jnp.concatenate(parts, axis=1)
    tri = split_words(full)
    blocks = jnp.stack([full[i:i + BLOCK, i:i + BLOCK] for i in range(0, total, BLOCK)])
    inv = split_words(block_inverses(jnp.tril(blocks, -1), pivots.reshape(-1, BLOCK)))

    block_ids = jnp.arange(sweeps, dtype=jnp.int32) * row_count + row_index
    keep = block_ids[:, None] > jnp.arange(panels, dtype=jnp.int32)[None, :]
    fac = jnp.where(keep[:, :, None, None], gathered, 0.0)
    fac = jnp.transpose(fac, (0, 3, 1, 2)).reshape(sweeps, rows, total)
    fac = split_words(fac)

    outs = None
    for k in range(CHUNKS):
        outs = chunk_call(k, CHUNKS, tri, inv, heads[k], fac, right_side, row_count, outs)
    return tuple(outs)


def solution(mesh):
    return jax.shard_map(
        per_device,
        mesh=mesh,
        in_specs=(P(None, None, "col", "row"), P(), P(None, "row", "col")),
        out_specs=(P(None, None, "col"), P(None, "row", "col")),
        check_vma=False,
    )
```

```python
import functools

import jax
import jax.numpy as jnp
from jax import lax
from jax.experimental import pallas as pl
from jax.experimental.pallas import tpu as pltpu
from jax.sharding import PartitionSpec as P

BLOCK = 128
BASE = 16
CHUNKS = 2
HIGHEST = lax.Precision.HIGHEST


def split(value):
    high = value.astype(jnp.bfloat16)
    low = (value - high.astype(jnp.float32)).astype(jnp.bfloat16)
    return high, low


def split_words(value):
    high = lax.reduce_precision(value, 8, 7)
    return high.astype(jnp.bfloat16), (value - high).astype(jnp.bfloat16)


def product(a_high, a_low, b_high, b_low):
    dot = functools.partial(jnp.dot, preferred_element_type=jnp.float32)
    return dot(a_high, b_high) + (dot(a_high, b_low) + dot(a_low, b_high))


def block_inverses(lower, diagonal):
    size = lower.shape[-1]
    mul = functools.partial(jnp.matmul, precision=HIGHEST)
    scaled = lower / diagonal[:, :, None]
    index = jnp.arange(size)
    eye = jnp.eye(size, dtype=jnp.float32)

    def same(width):
        return (index[:, None] // width) == (index[None, :] // width)

    power = jnp.where(same(BASE), -scaled, 0.0)
    inverse = eye + power
    width = 2
    while width < BASE:
        power = mul(power, power)
        inverse = inverse + mul(inverse, power)
        width *= 2
    width = BASE
    while width < size:
        off = jnp.where(same(2 * width) & ~same(width), scaled, 0.0)
        inverse = inverse - mul(mul(inverse, off), inverse)
        width *= 2
    return inverse / diagonal[:, None, :]


def chunk_kernel(panels, panel, row_count, tri_h, tri_l, inv_h, inv_l, rhs0, fac_h, fac_l, rhs, *rest):
    solved, trailing, x_high, x_low = rest[-4:]
    step = pl.program_id(0)
    total = panels * panel

    @pl.when(step == 0)
    def _():
        for i in range(total // BLOCK):
            lo, hi = i * BLOCK, (i + 1) * BLOCK
            p, at = lo // panel, lo % panel
            acc = rhs0[p, at:at + BLOCK, :]
            if i:
                acc = acc - product(tri_h[lo:hi, :lo], tri_l[lo:hi, :lo], x_high[:lo, :], x_low[:lo, :])
            a_high, a_low = split(acc)
            x = product(inv_h[i], inv_l[i], a_high, a_low)
            solved[p, at:at + BLOCK, :] = x
            b_high, b_low = split(x)
            x_high[lo:hi, :] = b_high
            x_low[lo:hi, :] = b_low

    @pl.when(step > 0)
    def _():
        trailing[0] = rhs[0] - product(fac_h[0], fac_l[0], x_high[...], x_low[...])


def chunk_call(index, chunks, tri, inv, rhs0, fac, right_side, row_count, previous):
    panels, panel = rhs0.shape[0], rhs0.shape[1]
    sweeps, rows, columns = right_side.shape
    width = columns // chunks
    total = panels * panel
    whole = lambda shape: pl.BlockSpec(shape, lambda s: (0,) * len(shape))
    sweep = lambda s: jnp.maximum(s - 1, 0)
    in_specs = [
        whole((total, total)), whole((total, total)),
        whole(inv[0].shape), whole(inv[1].shape),
        whole(rhs0.shape),
        pl.BlockSpec((1, rows, total), lambda s: (sweep(s), 0, 0)),
        pl.BlockSpec((1, rows, total), lambda s: (sweep(s), 0, 0)),
        pl.BlockSpec((1, rows, width), lambda s: (sweep(s), 0, index)),
    ]
    args = [*tri, *inv, rhs0, *fac, right_side]
    aliases = {}
    if previous is not None:
        in_specs += [pl.BlockSpec(memory_space=pl.ANY)] * 2
        aliases = {len(args): 0, len(args) + 1: 1}
        args += list(previous)
    return pl.pallas_call(
        functools.partial(chunk_kernel, panels, panel, row_count),
        grid=(sweeps + 1,),
        in_specs=in_specs,
        out_specs=[
            pl.BlockSpec((panels, panel, width), lambda s: (0, 0, index)),
            pl.BlockSpec((1, rows, width), lambda s: (sweep(s), 0, index)),
        ],
        out_shape=[
            jax.ShapeDtypeStruct((panels, panel, columns), jnp.float32),
            jax.ShapeDtypeStruct((sweeps, rows, columns), jnp.float32),
        ],
        scratch_shapes=[pltpu.VMEM((total, width), jnp.bfloat16)] * 2,
        input_output_aliases=aliases,
        compiler_params=pltpu.CompilerParams(vmem_limit_bytes=56 * 1024 * 1024),
        cost_estimate=pl.CostEstimate(
            flops=6 * (total * total // 2 + sweeps * rows * total) * width,
            bytes_accessed=4 * (total * total + sweeps * rows * total + 2 * sweeps * rows * width),
            transcendentals=0),
    )(*args)


def along_row(block, panels):
    row_index = lax.axis_index("row")
    row_count = lax.axis_size("row")
    ahead, held = [], block
    for step in range(row_count - 1):
        pairs = [(r, r + 1) for r in range(row_count - 1) if 0 <= r - step < panels]
        held = lax.ppermute(held, "row", pairs)
        ahead.append(held)
    back, held = [], block
    for step in range(panels - 1):
        pairs = [(r, r - 1) for r in range(1, row_count) if r + step < panels]
        held = lax.ppermute(held, "row", pairs)
        back.append(held)
    found = []
    for p in range(panels):
        value = block
        for r in range(row_count):
            if r != p:
                other = back[p - r - 1] if r < p else ahead[r - p - 1]
                value = jnp.where(row_index == r, other, value)
        found.append(value)
    return found


def per_device(factor_strip, pivots, right_side):
    row_index = lax.axis_index("row")
    row_count = lax.axis_size("row")
    sweeps, rows, columns = right_side.shape
    panels, panel = pivots.shape
    total = panels * panel

    shards = along_row(factor_strip[0], panels)
    local = jnp.concatenate(
        [shards[q][p] for p in range(panels) for q in range(p, panels)], axis=1)
    gathered = lax.all_gather(factor_strip, "col", axis=2, tiled=True)
    shared = lax.all_gather(local, "col", axis=0, tiled=True)
    width = columns // CHUNKS
    heads = [
        jnp.stack(along_row(right_side[0, :, k * width:(k + 1) * width], panels))
        for k in range(CHUNKS)
    ]

    parts, at = [], 0
    for p in range(panels):
        tall = total - p * panel
        parts.append(jnp.pad(shared[:, at:at + tall].T, ((p * panel, 0), (0, 0))))
        at += tall
    full = jnp.concatenate(parts, axis=1)
    tri = split_words(full)
    blocks = jnp.stack([full[i:i + BLOCK, i:i + BLOCK] for i in range(0, total, BLOCK)])
    inv = split_words(block_inverses(jnp.tril(blocks, -1), pivots.reshape(-1, BLOCK)))

    block_ids = jnp.arange(sweeps, dtype=jnp.int32) * row_count + row_index
    keep = block_ids[:, None] > jnp.arange(panels, dtype=jnp.int32)[None, :]
    fac = jnp.transpose(gathered, (0, 3, 1, 2)).reshape(sweeps, rows, total)
    fac = jnp.where(jnp.repeat(keep, panel, axis=1)[:, None, :], fac, 0.0)
    fac = split_words(fac)

    outs = None
    for k in range(CHUNKS):
        outs = chunk_call(k, CHUNKS, tri, inv, heads[k], fac, right_side, row_count, outs)
    return tuple(outs)


def solution(mesh):
    return jax.shard_map(
        per_device,
        mesh=mesh,
        in_specs=(P(None, None, "col", "row"), P(), P(None, "row", "col")),
        out_specs=(P(None, None, "col"), P(None, "row", "col")),
        check_vma=False,
    )
```
